32 devices in a mesh: gy: 16 (over z, y, core), var: 2 (over x).
Axes of the slice: x: 2, y: 2, z: 4, core: 2. Of those that a mesh axis runs over, the one named last changes fastest.
Arguments:
- field: float32 [32, 32, 512, 128], P('var', None, 'gy')
- factor_x: float32 [32, 16], replicated, may hold values from -1 to 1
- factor_y: float32 [512, 64], P('gy'), may hold values from -0.25 to 0.25
- factor_z: float32 [128, 64], replicated, may hold values from -0.5 to 0.5
- factor_v: float32 [32, 16], replicated, may hold values from -1 to 1
Outputs:
- proj_z: float32 [128, 128], replicated
- proj_v: float32 [32, 32], replicated
- core_rms: float32 [], replicated
The draws below stay inside these ranges and needn't reach their ends.
All inputs are finite; a program needn't handle non-finite values.
Results may differ from the reference program's by a relative error of at most 0.0003.
Values sent between devices are 32-bit elements; how exact they have to be, the bound alone decides.
A program may use at most 192 MiB of HBM per device.

```python
import jax
import jax.numpy as jnp
from jax import lax

NV = 32
NX = 32
NZ = 128
RX = 16
RY = 64
RZ = 64
RV = 16
NY = 512


def draw_field(key, part):
    key_var, key_cell, key_base = jax.random.split(key, 3)
    low = jnp.log(0.3)
    high = jnp.log(3.0)
    var_scale = jnp.exp(jax.random.uniform(key_var, (NV,), jnp.float32, low, high))
    cell_scale = jnp.exp(jax.random.uniform(key_cell, (NY, NZ), jnp.float32, low, high))
    rising = 1.0 + 2.0 * jnp.arange(NY, dtype=jnp.float32) / NY
    base = jax.random.normal(key_base, (NV, NX, NY, NZ), jnp.float32)
    scale = rising[:, None] * cell_scale
    return var_scale[:, None, None, None] * scale[None, None, :, :] * base


def levels(rng, dims, cuts, low, largest):
    def one(axis_at, parts):
        heights = jax.random.uniform(jax.random.fold_in(jax.random.fold_in(rng, 6), axis_at), (parts,), jnp.float32, low / len(cuts), largest / len(cuts))
        return jnp.repeat(jnp.exp(heights), dims[axis_at] // parts).reshape((-1,) + (1,) * (len(dims) - axis_at - 1))

    loudness = one(*cuts[0])
    for cut in cuts[1:]:
        loudness = loudness * one(*cut)
    return loudness


def noise(rng, dims, spread, limit, pieces=(), kind=jnp.bfloat16):
    factor_of = levels(rng, dims, pieces, -0.22, 0.18) if pieces else 1.0
    result = jax.random.normal(rng, dims, jnp.float32) * spread * factor_of
    return jnp.minimum(jnp.maximum(result, -limit), limit).astype(kind)


def setup_inputs(seed: int = 0) -> dict:
    keys = jax.random.split(jax.random.key(seed), 6)
    return {
        "field": draw_field(jax.random.fold_in(keys[5], 71), 0),
        "factor_x": noise(keys[1], (NX, RX), NX ** -0.5, 1.0, (), jnp.float32),
        "factor_y": noise(keys[2], (NY, RY), NY ** -0.5, 0.25, ((0, 16),), jnp.float32),
        "factor_z": noise(keys[3], (NZ, RZ), NZ ** -0.5, 0.5, (), jnp.float32),
        "factor_v": noise(keys[4], (NV, RV), NV ** -0.5, 1.0, (), jnp.float32),
    }


precise = lax.Precision.HIGHEST

def orth(mat):
    gram = jnp.dot(mat.T, mat, precision=precise)
    lower = jnp.linalg.cholesky(gram)
    return jax.scipy.linalg.solve_triangular(lower, mat.T, lower=True).T

def reference(field, factor_x, factor_y, factor_z, factor_v):
    along_x = jnp.einsum('vxyz,xa->vayz', field, factor_x, precision=precise)
    partial_value = jnp.einsum('vayz,yb->vabz', along_x, factor_y, precision=precise)
    wide_z = jnp.einsum('vabz,vc->cabz', partial_value, factor_v, precision=precise)
    small_core = jnp.einsum('cabz,zr->cabr', wide_z, factor_z, precision=precise)
    raw_z = jnp.einsum('cabz,cabr->zr', wide_z, small_core, precision=precise)
    new_z = orth(raw_z)
    proj_z = jnp.dot(new_z, new_z.T, precision=precise)
    wide_v = jnp.einsum('vabz,zr->vabr', partial_value, new_z, precision=precise)
    flat_v = wide_v.reshape(wide_v.shape[0], -1)
    gram_v = jnp.dot(flat_v, flat_v.T, precision=precise)
    new_v = orth(jnp.dot(gram_v, factor_v, precision=precise))
    proj_v = jnp.dot(new_v, new_v.T, precision=precise)
    core = jnp.dot(new_v.T, flat_v, precision=precise)
    core_rms = jnp.sqrt(jnp.mean(core * core))
    return (proj_z, proj_v, core_rms)
```

```python
import functools

import jax
import jax.numpy as jnp
from jax import lax
from jax.experimental import pallas as pl
from jax.experimental.pallas import tpu as pltpu
from jax.sharding import PartitionSpec as P

MESH = pl.DeviceIdType.MESH
F32 = jnp.float32
BF16 = jnp.bfloat16
N_CORE = 2
N_Z = 4


def exact(a, b, ca=1, cb=0):
    return lax.dot_general(
        a, b, (((ca,), (cb,)), ((), ())),
        precision=lax.Precision.HIGHEST, preferred_element_type=F32,
    )


def split(a):
    high = a.astype(BF16)
    return high, (a - high.astype(F32)).astype(BF16)


def three(a, b):
    def dot(p, q):
        return lax.dot_general(p, q, (((1,), (0,)), ((), ())), preferred_element_type=F32)
    return dot(a[0], b[0]) + (dot(a[0], b[1]) + dot(a[1], b[0]))


def iota(shape, dim):
    return lax.broadcasted_iota(jnp.int32, shape, dim)


def spread(shape, row_div, row_mod, col_div, col_mod):
    rows = (iota(shape, 0) // row_div) % row_mod
    cols = (iota(shape, 1) // col_div) % col_mod
    return (rows == cols).astype(F32)


def kron_eye(factor, eye):
    k, m = factor.shape
    tall = exact(spread((m * eye, m), eye, m, 1, m), factor, 1, 1)
    full = exact(tall, spread((k, k * eye), 1, k, eye, k))
    return full * spread((m * eye, k * eye), 1, eye, 1, eye)


def eye_kron(factor, eye):
    k, m = factor.shape
    tall = exact(spread((m * eye, m), 1, m, 1, m), factor, 1, 1)
    full = exact(tall, spread((k, k * eye), 1, k, 1, k))
    return full * spread((m * eye, k * eye), m, eye, k, eye)


def orth_rows(mat_t):
    rank = mat_t.shape[0]
    gram = exact(mat_t, mat_t, 1, 1)
    left = [gram[g:g + 8] for g in range(0, rank, 8)]
    right = [mat_t[g:g + 8] for g in range(0, rank, 8)]
    done = []
    for i in range(rank):
        g, k = i // 8, i % 8
        row_l, row_r = left[g][k:k + 1], right[g][k:k + 1]
        pivot = row_l[:, i:i + 1]
        inverse = 1.0 / pivot
        scaled_l, scaled_r = row_l * inverse, row_r * inverse
        done.append(row_r * lax.rsqrt(pivot))
        for h in range(g, rank // 8):
            col = left[h][:, i:i + 1]
            if h == g:
                col = jnp.where(iota((8, 1), 0) > k, col, 0.0)
            left[h] = left[h] - col * scaled_l
            right[h] = right[h] - col * scaled_r
    return jnp.concatenate(done, axis=0)


def kernel(
    n_y, n_var, core_size,
    field, fx_ref, fy_ref, fz_ref, fv_ref,
    proj_z_ref, proj_v_ref, rms_ref,
    fbuf, ax, axr, fy_own, fy_sib, acc,
    y_right, y_left, z_right, z_left, pown,
    red_z, red_v,
    in_sem, fy_sem, core_sem, y_sem, z_sem, x_sem, red_sem,
):
    slabs, per, rows = acc.shape[0], acc.shape[1], acc.shape[4]
    nx = fx_ref.shape[0]
    ny_loc = fy_ref.shape[0]
    ra, rb = fx_ref.shape[1], fy_ref.shape[1]
    half_a = ra // N_CORE
    nz = field.shape[3]
    at = lax.axis_index("gy")
    var = lax.axis_index("var")
    core = at % N_CORE
    y = (at // N_CORE) % n_y
    z = at // (N_CORE * n_y)

    def device(pz=z, py=y, pc=core, pv=var):
        return ((pz * n_y + py) * N_CORE + pc, pv)

    sibling = device(pc=1 - core)
    axes = [
        (N_CORE, core, lambda k: device(pc=k)),
        (n_var, var, lambda k: device(pv=k)),
        (n_y, y, lambda k: device(py=k)),
        (N_Z, z, lambda k: device(pz=k)),
    ]

    loads = [
        pltpu.make_async_copy(field.at[pl.ds(s * per, per)], fbuf.at[s], in_sem.at[s])
        for s in range(slabs)
    ]
    for load in loads:
        load.start()

    barrier = pltpu.get_barrier_semaphore()
    others = 0
    for n, me, who in axes:
        for d in range(1, n):
            pl.semaphore_signal(
                barrier, inc=1, device_id=who(lax.rem(me + d, n)), device_id_type=MESH)
            others += 1

    w_x = split(kron_eye(fx_ref[...], 8))
    fy_own[...] = jnp.zeros_like(fy_own)
    fy_own[:, :rb] = fy_ref[...]
    pl.semaphore_wait(barrier, others)

    def remote(src, dst, sems, index, where):
        return pltpu.make_async_remote_copy(
            src_ref=src, dst_ref=dst,
            send_sem=sems.at[(0,) + index], recv_sem=sems.at[(1,) + index],
            device_id=where, device_id_type=MESH)

    fy_copy = remote(fy_own, fy_sib, fy_sem, (0,), sibling)
    fy_copy.start()

    def core_copy(s):
        return remote(ax.at[1 - core, s], axr.at[s], core_sem, (s,), sibling)

    for s in range(slabs):
        loads[s].wait()
        for g in range(0, ny_loc, 8):
            block = jnp.concatenate(
                [fbuf[s, v, :, g:g + 8, :].reshape(nx * 8, nz) for v in range(per)], axis=1)
            out = three(w_x, split(block))
            for h in range(N_CORE):
                for v in range(per):
                    piece = out[h * half_a * 8:(h + 1) * half_a * 8, v * nz:(v + 1) * nz]
                    ax[h, s, v, :, g:g + 8, :] = piece.reshape(half_a, 8, nz)
        core_copy(s).start()

    w_own = split(eye_kron(fy_own[:, :rb], half_a))
    fy_copy.wait()
    w_sib = split(eye_kron(fy_sib[:, :rb], half_a))

    def line(s, hop, n, pos, view, right, left, sems, who):
        @pl.when(pos == hop)
        def _():
            for j in range(n - 1, hop - 1, -1):
                if hop > 0:
                    remote(view(acc, s, j), view(right, s, j), sems, (0, s, j), who(hop - 1)).wait_recv()
                    view(acc, s, j)[...] += view(right, s, j)[...]
                if j > hop:
                    remote(view(acc, s, j), view(right, s, j), sems, (0, s, j), who(hop + 1)).start()
        mine = n - 1 - hop

        @pl.when(pos == mine)
        def _():
            for j in range(0, mine + 1):
                if hop > 0:
                    remote(view(acc, s, j), view(left, s, j), sems, (1, s, j), who(mine + 1)).wait_recv()
                    view(acc, s, j)[...] += view(left, s, j)[...]
                if j < mine:
                    remote(view(acc, s, j), view(left, s, j), sems, (1, s, j), who(mine - 1)).start()

    def line_end(n, pos, view, right, left, sems, who):
        for p in range(n):
            @pl.when(pos == p)
            def _():
                for s in range(slabs):
                    for j in range(p + 1, n):
                        remote(view(acc, s, j), view(right, s, j), sems, (0, s, j), who(p + 1)).wait_send()
                    for j in range(p):
                        remote(view(acc, s, j), view(left, s, j), sems, (1, s, j), who(p - 1)).wait_send()

    def view_y(ref, s, j):
        return ref.at[s, :, j]

    def view_z(ref, s, j):
        if ref is acc:
            return ref.at[s, :, y, j]
        return ref.at[s, :, j]

    y_args = (n_y, y, view_y, y_right, y_left, y_sem, axes[2][2])
    z_args = (N_Z, z, view_z, z_right, z_left, z_sem, axes[3][2])
    part = rows // n_var

    def x_copy(s, to, slot, src_var):
        return remote(acc.at[s, :, y, z, pl.ds(pl.multiple_of(to * part, part), part)],
                      pown.at[src_var, s], x_sem, (s, slot), device(pv=to))

    for t in range(slabs + n_y - 1 + N_Z - 1):
        if t < slabs:
            core_copy(t).wait_recv()
            own = jnp.concatenate(
                [ax[core, t, v].reshape(half_a * ny_loc, nz) for v in range(per)], axis=1)
            sib = jnp.concatenate(
                [axr[t, v].reshape(half_a * ny_loc, nz) for v in range(per)], axis=1)
            out = three(w_own, split(own)) + three(w_sib, split(sib))
            for v in range(per):
                acc[t, v] = out[:, v * nz:(v + 1) * nz].reshape(n_y, N_Z, rows, nz)
        for hop in range(n_y):
            if 0 <= t - hop < slabs:
                line(t - hop, hop, *y_args)
        for hop in range(N_Z):
            s = t - (n_y - 1) - hop
            if 0 <= s < slabs:
                line(s, hop, *z_args)
                if hop == N_Z - 1:
                    for d in range(1, n_var):
                        x_copy(s, lax.rem(var + d, n_var), d, var).start()
                    keep = pl.ds(pl.multiple_of(var * part, part), part)
                    pown[var, s] = acc[s, :, y, z, keep, :]

    w_v = kron_eye(fv_ref[...], 8)
    for s in range(slabs):
        for d in range(1, n_var):
            x_copy(s, lax.rem(var + d, n_var), d, lax.rem(var + n_var - d, n_var)).wait()

    def octet(o):
        return pown[:, :, :, o:o + 8, :].reshape(n_var * slabs * per * 8, nz)

    gram_z = jnp.zeros((nz, nz), F32)
    for o in range(0, part, 8):
        wide = exact(w_v, octet(o))
        gram_z += exact(wide.T, wide)
    raw = exact(gram_z, fz_ref[...])

    def total(value, buf, base):
        first = 0
        for n, me, who in axes:
            buf[first + me] = value
            copies = []
            for d in range(1, n):
                copies.append(remote(
                    buf.at[first + me], buf.at[first + me], red_sem,
                    (base + first + d,), who(lax.rem(me + d, n))))
                copies[-1].start()
            for copy in copies:
                copy.wait()
            value = buf[first]
            for k in range(1, n):
                value = value + buf[first + k]
            first += n
        return value

    slots = sum(n for n, _, _ in axes)
    half = nz // 2
    packed = total(jnp.concatenate([raw[:half], raw[half:]], axis=1), red_z, 0)
    width = raw.shape[1]
    raw = jnp.concatenate([packed[:, :width], packed[:, width:]], axis=0)
    basis_t = orth_rows(raw.T)
    proj_z_ref[...] = exact(basis_t.T, basis_t)

    nv = n_var * slabs * per
    cross = jnp.zeros((nv * 8, nv * 8), F32)
    for o in range(0, part, 8):
        wide = exact(octet(o), basis_t, 1, 1)
        cross += exact(wide, wide, 1, 1)
    cross = cross * spread((nv * 8, nv * 8), 1, 8, 1, 8)
    fold = exact(spread((nv, nv * 8), 1, nv, 8, nv), cross)
    gram_v = exact(fold, spread((nv * 8, 128), 8, nv, 1, 128))
    gram_v = total(gram_v, red_v, slots)[:, :nv]
    new_t = orth_rows(exact(gram_v, fv_ref[...]).T)
    proj_v_ref[...] = exact(new_t.T, new_t)
    energy = exact(new_t, gram_v) * new_t
    rms_ref[...] = jnp.sqrt(
        jnp.sum(jnp.sum(energy, axis=1, keepdims=True), axis=0, keepdims=True) * (1.0 / core_size))

    for s in range(slabs):
        core_copy(s).wait_send()
    line_end(*y_args)
    line_end(*z_args)


def per_device(n_gy, n_var, field, fx, fy, fz, fv):
    n_y = n_gy // (N_Z * N_CORE)
    v_loc, nx, ny_loc, nz = field.shape
    per = 2
    slabs = v_loc // per
    ra, rb = fx.shape[1], fy.shape[1]
    half_a = ra // N_CORE
    rows = half_a * rb // (n_y * N_Z)
    part = rows // n_var
    nv = fv.shape[0]
    slots = N_CORE + n_var + n_y + N_Z
    core_size = fv.shape[1] * ra * rb * fz.shape[1]
    vmem = pl.BlockSpec(memory_space=pltpu.VMEM)
    big = (slabs, per, n_y, N_Z, rows, nz)
    small = (slabs, per, N_Z, rows, nz)
    dma = pltpu.SemaphoreType.DMA
    proj_z, proj_v, rms = pl.pallas_call(
        functools.partial(kernel, n_y, n_var, core_size),
        out_shape=(
            jax.ShapeDtypeStruct((nz, nz), F32),
            jax.ShapeDtypeStruct((nv, nv), F32),
            jax.ShapeDtypeStruct((1, 1), F32),
        ),
        in_specs=[pl.BlockSpec(memory_space=pl.ANY), vmem, vmem, vmem, vmem],
        out_specs=(vmem, vmem, vmem),
        scratch_shapes=[
            pltpu.VMEM((slabs, per, nx, ny_loc, nz), F32),
            pltpu.VMEM((N_CORE, slabs, per, half_a, ny_loc, nz), F32),
            pltpu.VMEM((slabs, per, half_a, ny_loc, nz), F32),
            pltpu.VMEM((ny_loc, 128), F32),
            pltpu.VMEM((ny_loc, 128), F32),
            pltpu.VMEM(big, F32),
            pltpu.VMEM(big, F32),
            pltpu.VMEM(big, F32),
            pltpu.VMEM(small, F32),
            pltpu.VMEM(small, F32),
            pltpu.VMEM((n_var, slabs, per, part, nz), F32),
            pltpu.VMEM((slots, nz // 2, 2 * fz.shape[1]), F32),
            pltpu.VMEM((slots, nv, 128), F32),
            dma((slabs,)),
            dma((2, 1)),
            dma((2, slabs)),
            dma((2, 2, slabs, n_y)),
            dma((2, 2, slabs, N_Z)),
            dma((2, slabs, n_var)),
            dma((2, 2 * slots)),
        ],
        compiler_params=pltpu.CompilerParams(
            collective_id=0, has_side_effects=True, vmem_limit_bytes=52 * 2**20),
        cost_estimate=pl.CostEstimate(
            flops=10**10, bytes_accessed=4 * v_loc * nx * ny_loc * nz, transcendentals=0),
    )(field, fx, fy, fz, fv)
    return proj_z, proj_v, rms[0, 0]


def solution(mesh):
    in_specs = (P("var", None, "gy", None), P(), P("gy", None), P(), P())
    return jax.shard_map(
        functools.partial(per_device, mesh.shape["gy"], mesh.shape["var"]),
        mesh=mesh, in_specs=in_specs, out_specs=(P(), P(), P()), check_vma=False,
    )
```

```python
import functools

import jax
import jax.numpy as jnp
from jax import lax
from jax.experimental import pallas as pl
from jax.experimental.pallas import tpu as pltpu
from jax.sharding import PartitionSpec as P

MESH = pl.DeviceIdType.MESH
F32 = jnp.float32
BF16 = jnp.bfloat16
N_CORE = 2
N_Z = 4


def exact(a, b, ca=1, cb=0):
    return lax.dot_general(
        a, b, (((ca,), (cb,)), ((), ())),
        precision=lax.Precision.HIGHEST, preferred_element_type=F32,
    )


def split(a):
    high = a.astype(BF16)
    return high, (a - high.astype(F32)).astype(BF16)


def three(a, b, cb=0):
    def dot(p, q):
        return lax.dot_general(p, q, (((1,), (cb,)), ((), ())), preferred_element_type=F32)
    return dot(a[0], b[0]) + (dot(a[0], b[1]) + dot(a[1], b[0]))


def iota(shape, dim):
    return lax.broadcasted_iota(jnp.int32, shape, dim)


def spread(shape, row_div, row_mod, col_div, col_mod):
    rows = (iota(shape, 0) // row_div) % row_mod
    cols = (iota(shape, 1) // col_div) % col_mod
    return (rows == cols).astype(F32)


def kron_eye(factor_t, eye):
    m, k = factor_t.shape
    tall = exact(spread((m * eye, m), eye, m, 1, m), factor_t)
    full = exact(tall, spread((k, k * eye), 1, k, eye, k))
    return full * spread((m * eye, k * eye), 1, eye, 1, eye)


def eye_kron(factor, eye):
    k, m = factor.shape
    tall = exact(spread((m * eye, m), 1, m, 1, m), factor, 1, 1)
    full = exact(tall, spread((k, k * eye), 1, k, 1, k))
    return full * spread((m * eye, k * eye), m, eye, k, eye)


def orth_rows(mat_t):
    rank = mat_t.shape[0]
    gram = exact(mat_t, mat_t, 1, 1)
    left = [gram[g:g + 8] for g in range(0, rank, 8)]
    right = [mat_t[g:g + 8] for g in range(0, rank, 8)]
    done = []
    for i in range(rank):
        g, k = i // 8, i % 8
        row_l, row_r = left[g][k:k + 1], right[g][k:k + 1]
        pivot = row_l[:, i:i + 1]
        inverse = 1.0 / pivot
        scaled_l, scaled_r = row_l * inverse, row_r * inverse
        done.append(row_r * lax.rsqrt(pivot))
        for h in range(g, rank // 8):
            col = left[h][:, i:i + 1]
            if h == g:
                col = jnp.where(iota((8, 1), 0) > k, col, 0.0)
            left[h] = left[h] - col * scaled_l
            right[h] = right[h] - col * scaled_r
    return jnp.concatenate(done, axis=0)


def kernel(
    n_y, n_var, core_size,
    field, fx_arg, fy_arg, fz_arg, fv_arg,
    proj_z_ref, proj_v_ref, rms_ref,
    fbuf, ax, axr, fy_own, fy_sib, acc,
    early_right, early_left, late_right, late_left, pown,
    red_z, red_v, fx_ref, fy_ref, fz_ref, fv_ref,
    in_sem, arg_sem, fy_sem, core_sem, y_sem, z_sem, x_sem, red_sem,
):
    slabs, per, rows = acc.shape[0], acc.shape[1], acc.shape[4]
    ra, nx = fx_ref.shape
    ny_loc, rb = fy_ref.shape
    half_a = ra // N_CORE
    nz = field.shape[3]
    at = lax.axis_index("gy")
    var = lax.axis_index("var")
    core = at % N_CORE
    y = (at // N_CORE) % n_y
    z = at // (N_CORE * n_y)

    def device(pz=z, py=y, pc=core, pv=var):
        return ((pz * n_y + py) * N_CORE + pc, pv)

    sibling = device(pc=1 - core)
    pair = (N_CORE * n_var, var * N_CORE + core,
            lambda k: device(pc=k % N_CORE, pv=k // N_CORE))
    plane = (N_CORE * n_var * n_y, (y * n_var + var) * N_CORE + core,
             lambda k: device(pc=k % N_CORE, pv=(k // N_CORE) % n_var, py=k // (N_CORE * n_var)))
    along_y = (n_y, y, lambda k: device(py=k))
    along_z = (N_Z, z, lambda k: device(pz=k))

    loads = [
        pltpu.make_async_copy(field.at[pl.ds(s * per, per)], fbuf.at[s], in_sem.at[s])
        for s in range(slabs)
    ]
    params = [
        pltpu.make_async_copy(src, dst, arg_sem.at[i])
        for i, (src, dst) in enumerate(
            [(fx_arg, fx_ref), (fy_arg, fy_ref), (fz_arg, fz_ref), (fv_arg, fv_ref)])
    ]
    for load in params + loads:
        load.start()

    barrier = pltpu.get_barrier_semaphore()
    others = 0
    for n, me, who in (plane, along_z):
        for d in range(1, n):
            pl.semaphore_signal(
                barrier, inc=1, device_id=who(lax.rem(me + d, n)), device_id_type=MESH)
            others += 1

    for load in params:
        load.wait()
    w_x = split(kron_eye(fx_ref[...], 8))
    fy_own[...] = jnp.zeros_like(fy_own)
    fy_own[:, :rb] = fy_ref[...]
    pl.semaphore_wait(barrier, others)

    def remote(src, dst, sems, index, where):
        return pltpu.make_async_remote_copy(
            src_ref=src, dst_ref=dst,
            send_sem=sems.at[(0,) + index], recv_sem=sems.at[(1,) + index],
            device_id=where, device_id_type=MESH)

    fy_copy = remote(fy_own, fy_sib, fy_sem, (0,), sibling)
    fy_copy.start()

    def core_copy(s):
        return remote(ax.at[1 - core, s], axr.at[s], core_sem, (s,), sibling)

    def stage_x(s):
        loads[s].wait()
        for g in range(0, ny_loc, 8):
            block = jnp.concatenate(
                [fbuf[s, v, :, g:g + 8, :].reshape(nx * 8, nz) for v in range(per)], axis=1)
            out = three(w_x, split(block))
            for h in range(N_CORE):
                for v in range(per):
                    piece = out[h * half_a * 8:(h + 1) * half_a * 8, v * nz:(v + 1) * nz]
                    ax[h, s, v, :, g:g + 8, :] = piece.reshape(half_a, 8, nz)
        core_copy(s).start()

    def line(s, hop, n, pos, view, right, left, sems, who):
        @pl.when(pos == hop)
        def _():
            for j in range(n - 1, hop - 1, -1):
                if hop > 0:
                    remote(view(acc, s, j), view(right, s, j), sems, (0, s, j), who(hop - 1)).wait_recv()
                    view(acc, s, j)[...] += view(right, s, j)[...]
                if j > hop:
                    remote(view(acc, s, j), view(right, s, j), sems, (0, s, j), who(hop + 1)).start()
        mine = n - 1 - hop

        @pl.when(pos == mine)
        def _():
            for j in range(0, mine + 1):
                if hop > 0:
                    remote(view(acc, s, j), view(left, s, j), sems, (1, s, j), who(mine + 1)).wait_recv()
                    view(acc, s, j)[...] += view(left, s, j)[...]
                if j < mine:
                    remote(view(acc, s, j), view(left, s, j), sems, (1, s, j), who(mine - 1)).start()

    def line_end(args_of):
        n, pos = args_of(0)[:2]
        for p in range(n):
            @pl.when(pos == p)
            def _():
                for s in range(slabs):
                    _, _, view, right, left, sems, who = args_of(s)
                    for j in range(p + 1, n):
                        remote(view(acc, s, j), view(right, s, j), sems, (0, s, j), who(p + 1)).wait_send()
                    for j in range(p):
                        remote(view(acc, s, j), view(left, s, j), sems, (1, s, j), who(p - 1)).wait_send()

    def z_first(s):
        return s < slabs // 8

    def view_y(ref, s, j):
        if ref is acc and z_first(s):
            return ref.at[s, :, j, z]
        return ref.at[s, :, j]

    def view_z(ref, s, j):
        if not z_first(s):
            return ref.at[s, :, y, j] if ref is acc else ref.at[s, :, j]
        return ref.at[s, :, :, j]

    def y_args(s):
        bufs = (late_right, late_left) if z_first(s) else (early_right, early_left)
        return (n_y, y, view_y) + bufs + (y_sem, along_y[2])

    def z_args(s):
        bufs = (early_right, early_left) if z_first(s) else (late_right, late_left)
        return (N_Z, z, view_z) + bufs + (z_sem, along_z[2])
    part = rows // n_var

    def x_copy(s, to, slot, src_var):
        return remote(acc.at[s, :, y, z, pl.ds(pl.multiple_of(to * part, part), part)],
                      pown.at[src_var, s], x_sem, (s, slot), device(pv=to))

    def stage_y(s):
        core_copy(s).wait_recv()
        own = jnp.concatenate(
            [ax[core, s, v].reshape(half_a * ny_loc, nz) for v in range(per)], axis=1)
        sib = jnp.concatenate(
            [axr[s, v].reshape(half_a * ny_loc, nz) for v in range(per)], axis=1)
        out = three(w_own, split(own)) + three(w_sib, split(sib))
        for v in range(per):
            acc[s, v] = out[:, v * nz:(v + 1) * nz].reshape(n_y, N_Z, rows, nz)

    ahead = 2
    for s in range(ahead):
        stage_x(s)
    w_own = split(eye_kron(fy_own[:, :rb], half_a))
    fy_copy.wait()
    w_sib = split(eye_kron(fy_sib[:, :rb], half_a))
    for t in range(slabs + n_y + N_Z):
        if t + ahead < slabs:
            stage_x(t + ahead)
        if t < slabs:
            stage_y(t)
        if t == slabs - 1:
            w_v = split(kron_eye(fv_ref[...], 8))
        for s in range(min(t, slabs - 1), -1, -1):
            lag = t - s
            stages = [z_args(s), y_args(s)] if z_first(s) else [y_args(s), z_args(s)]
            n_first, n_second = stages[0][0], stages[1][0]
            if lag == 0:
                line(s, 0, *stages[0])
            if 2 <= lag <= n_first:
                line(s, lag - 1, *stages[0])
            if n_first <= lag < n_first + n_second:
                line(s, lag - n_first, *stages[1])
            if lag == n_first + n_second - 1:
                for d in range(1, n_var):
                    x_copy(s, lax.rem(var + d, n_var), d, var).start()
                keep = pl.ds(pl.multiple_of(var * part, part), part)
                pown[var, s] = acc[s, :, y, z, keep, :]

    for s in range(slabs):
        for d in range(1, n_var):
            x_copy(s, lax.rem(var + d, n_var), d, lax.rem(var + n_var - d, n_var)).wait()

    nv = n_var * slabs * per
    octets = [pown[:, :, :, o:o + 8, :].reshape(nv * 8, nz) for o in range(0, part, 8)]
    wide = three(w_v, split(jnp.concatenate(octets, axis=1)))
    wide = jnp.concatenate(
        [wide[:, k * nz:(k + 1) * nz] for k in range(len(octets))], axis=0)
    raw = exact(three(split(wide.T), split(wide)), fz_ref[...], 1, 1)

    def total(value, groups, buf, base):
        first = 0
        for n, me, who in groups:
            buf[first + me] = value
            copies = []
            for d in range(1, n):
                copies.append(remote(
                    buf.at[first + me], buf.at[first + me], red_sem,
                    (base + first + d,), who(lax.rem(me + d, n))))
                copies[-1].start()
            for copy in copies:
                copy.wait()
            value = buf[first]
            for k in range(1, n):
                value = value + buf[first + k]
            first += n
        return value

    half = nz // 2
    packed = total(
        jnp.concatenate([raw[:half], raw[half:]], axis=1), (pair, along_y, along_z), red_z, 0)
    width = raw.shape[1]
    raw = jnp.concatenate([packed[:, :width], packed[:, width:]], axis=0)
    basis_t = orth_rows(raw.T)

    tall = three(split(jnp.concatenate(octets, axis=0)), split(basis_t), 1)
    wide = split(jnp.concatenate(
        [tall[k * nv * 8:(k + 1) * nv * 8] for k in range(len(octets))], axis=1))
    cross = three(wide, wide, 1)
    cross = cross * spread((nv * 8, nv * 8), 1, 8, 1, 8)
    fold = exact(spread((nv, nv * 8), 1, nv, 8, nv), cross)
    gram_v = exact(fold, spread((nv * 8, nv), 8, nv, 1, nv))
    packed = total(
        jnp.concatenate([gram_v[k:k + 8] for k in range(0, nv, 8)], axis=1),
        (plane, along_z), red_v, red_z.shape[0])
    gram_v = jnp.concatenate([packed[:, k * nv:(k + 1) * nv] for k in range(nv // 8)], axis=0)
    proj_z_ref[...] = exact(basis_t.T, basis_t)
    new_t = orth_rows(exact(fv_ref[...], gram_v))
    proj_v_ref[...] = exact(new_t.T, new_t)
    energy = exact(new_t, gram_v) * new_t
    rms_ref[...] = jnp.sqrt(
        jnp.sum(jnp.sum(energy, axis=1, keepdims=True), axis=0, keepdims=True) * (1.0 / core_size))

    for s in range(slabs):
        core_copy(s).wait_send()
    line_end(y_args)
    line_end(z_args)


def per_device(n_gy, n_var, field, fx, fy, fz, fv):
    n_y = n_gy // (N_Z * N_CORE)
    v_loc, nx, ny_loc, nz = field.shape
    per = 1
    slabs = v_loc // per
    ra, rb = fx.shape[1], fy.shape[1]
    half_a = ra // N_CORE
    rows = half_a * rb // (n_y * N_Z)
    part = rows // n_var
    nv = fv.shape[0]
    slots_z = N_CORE * n_var + n_y + N_Z
    slots_v = N_CORE * n_var * n_y + N_Z
    core_size = fv.shape[1] * ra * rb * fz.shape[1]
    vmem = pl.BlockSpec(memory_space=pltpu.VMEM)
    big = (slabs, per, n_y, N_Z, rows, nz)
    small = (slabs, per, N_Z, rows, nz)
    dma = pltpu.SemaphoreType.DMA
    proj_z, proj_v, rms = pl.pallas_call(
        functools.partial(kernel, n_y, n_var, core_size),
        out_shape=(
            jax.ShapeDtypeStruct((nz, nz), F32),
            jax.ShapeDtypeStruct((nv, nv), F32),
            jax.ShapeDtypeStruct((1, 1), F32),
        ),
        in_specs=[pl.BlockSpec(memory_space=pl.ANY)] * 5,
        out_specs=(vmem, vmem, vmem),
        scratch_shapes=[
            pltpu.VMEM((slabs, per, nx, ny_loc, nz), F32),
            pltpu.VMEM((N_CORE, slabs, per, half_a, ny_loc, nz), F32),
            pltpu.VMEM((slabs, per, half_a, ny_loc, nz), F32),
            pltpu.VMEM((ny_loc, 128), F32),
            pltpu.VMEM((ny_loc, 128), F32),
            pltpu.VMEM(big, F32),
            pltpu.VMEM(big, F32),
            pltpu.VMEM(big, F32),
            pltpu.VMEM(small, F32),
            pltpu.VMEM(small, F32),
            pltpu.VMEM((n_var, slabs, per, part, nz), F32),
            pltpu.VMEM((slots_z, nz // 2, 2 * fz.shape[1]), F32),
            pltpu.VMEM((slots_v, 8, nv * nv // 8), F32),
            pltpu.VMEM(fx.shape[::-1], F32),
            pltpu.VMEM(fy.shape, F32),
            pltpu.VMEM(fz.shape[::-1], F32),
            pltpu.VMEM(fv.shape[::-1], F32),
            dma((slabs,)),
            dma((4,)),
            dma((2, 1)),
            dma((2, slabs)),
            dma((2, 2, slabs, n_y)),
            dma((2, 2, slabs, N_Z)),
            dma((2, slabs, n_var)),
            dma((2, slots_z + slots_v)),
        ],
        compiler_params=pltpu.CompilerParams(
            collective_id=0, has_side_effects=True, vmem_limit_bytes=52 * 2**20),
        cost_estimate=pl.CostEstimate(
            flops=10**10, bytes_accessed=4 * v_loc * nx * ny_loc * nz, transcendentals=0),
    )(field, fx.T, fy, fz.T, fv.T)
    return proj_z, proj_v, rms[0, 0]


def solution(mesh):
    in_specs = (P("var", None, "gy", None), P(), P("gy", None), P(), P())
    return jax.shard_map(
        functools.partial(per_device, mesh.shape["gy"], mesh.shape["var"]),
        mesh=mesh, in_specs=in_specs, out_specs=(P(), P(), P()), check_vma=False,
    )
```

```python
import functools

import jax
import jax.numpy as jnp
from jax import lax
from jax.experimental import pallas as pl
from jax.experimental.pallas import tpu as pltpu
from jax.sharding import PartitionSpec as P

MESH = pl.DeviceIdType.MESH
F32 = jnp.float32
BF16 = jnp.bfloat16
N_CORE = 2
N_Z = 4


def exact(a, b, ca=1, cb=0):
    return lax.dot_general(
        a, b, (((ca,), (cb,)), ((), ())),
        precision=lax.Precision.HIGHEST, preferred_element_type=F32,
    )


def split(a):
    high = a.astype(BF16)
    return high, (a - high.astype(F32)).astype(BF16)


def three(a, b, cb=0):
    def dot(p, q):
        return lax.dot_general(p, q, (((1,), (cb,)), ((), ())), preferred_element_type=F32)
    return dot(a[0], b[0]) + (dot(a[0], b[1]) + dot(a[1], b[0]))


def iota(shape, dim):
    return lax.broadcasted_iota(jnp.int32, shape, dim)


def spread(shape, row_div, row_mod, col_div, col_mod):
    rows = (iota(shape, 0) // row_div) % row_mod
    cols = (iota(shape, 1) // col_div) % col_mod
    return (rows == cols).astype(F32)


def kron_eye(factor_t, eye):
    m, k = factor_t.shape
    tall = exact(spread((m * eye, m), eye, m, 1, m), factor_t)
    full = exact(tall, spread((k, k * eye), 1, k, eye, k))
    return full * spread((m * eye, k * eye), 1, eye, 1, eye)


def eye_kron(factor, eye):
    k, m = factor.shape
    tall = exact(spread((m * eye, m), 1, m, 1, m), factor, 1, 1)
    full = exact(tall, spread((k, k * eye), 1, k, 1, k))
    return full * spread((m * eye, k * eye), m, eye, k, eye)


def orth_rows(mat_t):
    rank = mat_t.shape[0]
    gram = exact(mat_t, mat_t, 1, 1)
    left = [gram[g:g + 8] for g in range(0, rank, 8)]
    right = [mat_t[g:g + 8] for g in range(0, rank, 8)]
    done = []
    for i in range(rank):
        g, k = i // 8, i % 8
        row_l, row_r = left[g][k:k + 1], right[g][k:k + 1]
        pivot = row_l[:, i:i + 1]
        inverse = 1.0 / pivot
        scaled_l, scaled_r = row_l * inverse, row_r * inverse
        done.append(row_r * lax.rsqrt(pivot))
        for h in range(g, rank // 8):
            col = left[h][:, i:i + 1]
            if h == g:
                col = jnp.where(iota((8, 1), 0) > k, col, 0.0)
            left[h] = left[h] - col * scaled_l
            right[h] = right[h] - col * scaled_r
    return jnp.concatenate(done, axis=0)


def each(count, body, first=0):
    def step(t, carry):
        body(t)
        return carry
    lax.fori_loop(first, count, step, 0)


def kernel(
    n_y, n_var, core_size,
    field, fx_arg, fy_arg, fz_arg, fv_arg,
    proj_z_ref, proj_v_ref, rms_ref,
    fbuf, ax, axr, fy_own, fy_sib, acc,
    early_right, early_left, late_right, late_left, pown,
    red_z, red_v, fx_ref, fy_ref, fz_ref, fv_ref,
    in_sem, arg_sem, fy_sem, core_sem, y_sem, z_sem, x_sem, red_sem,
):
    slabs, per, rows = acc.shape[0], acc.shape[1], acc.shape[4]
    ra, nx = fx_ref.shape
    ny_loc, rb = fy_ref.shape
    half_a = ra // N_CORE
    nz = field.shape[3]
    at = lax.axis_index("gy")
    var = lax.axis_index("var")
    core = at % N_CORE
    y = (at // N_CORE) % n_y
    z = at // (N_CORE * n_y)

    def device(pz=z, py=y, pc=core, pv=var):
        return ((pz * n_y + py) * N_CORE + pc, pv)

    sibling = device(pc=1 - core)
    pair = (N_CORE * n_var, var * N_CORE + core,
            lambda k: device(pc=k % N_CORE, pv=k // N_CORE))
    plane = (N_CORE * n_var * n_y, (y * n_var + var) * N_CORE + core,
             lambda k: device(pc=k % N_CORE, pv=(k // N_CORE) % n_var, py=k // (N_CORE * n_var)))
    along_y = (n_y, y, lambda k: device(py=k))
    along_z = (N_Z, z, lambda k: device(pz=k))

    def load_of(s):
        return pltpu.make_async_copy(field.at[pl.ds(s * per, per)], fbuf.at[s], in_sem.at[s])

    params = [
        pltpu.make_async_copy(src, dst, arg_sem.at[i])
        for i, (src, dst) in enumerate(
            [(fx_arg, fx_ref), (fy_arg, fy_ref), (fz_arg, fz_ref), (fv_arg, fv_ref)])
    ]
    for load in params:
        load.start()
    each(slabs, lambda s: load_of(s).start())

    barrier = pltpu.get_barrier_semaphore()
    others = 0
    for n, me, who in (plane, along_z):
        for d in range(1, n):
            pl.semaphore_signal(
                barrier, inc=1, device_id=who(lax.rem(me + d, n)), device_id_type=MESH)
            others += 1

    for load in params:
        load.wait()
    w_x = split(kron_eye(fx_ref[...], 8))
    fy_own[...] = jnp.zeros_like(fy_own)
    fy_own[:, :rb] = fy_ref[...]
    pl.semaphore_wait(barrier, others)

    def remote(src, dst, sems, index, where):
        return pltpu.make_async_remote_copy(
            src_ref=src, dst_ref=dst,
            send_sem=sems.at[(0,) + index], recv_sem=sems.at[(1,) + index],
            device_id=where, device_id_type=MESH)

    fy_copy = remote(fy_own, fy_sib, fy_sem, (0,), sibling)
    fy_copy.start()

    def core_copy(s):
        return remote(ax.at[1 - core, s], axr.at[s], core_sem, (s,), sibling)

    def stage_x(s):
        load_of(s).wait()
        for g in range(0, ny_loc, 8):
            block = jnp.concatenate(
                [fbuf[s, v, :, g:g + 8, :].reshape(nx * 8, nz) for v in range(per)], axis=1)
            out = three(w_x, split(block))
            for h in range(N_CORE):
                for v in range(per):
                    piece = out[h * half_a * 8:(h + 1) * half_a * 8, v * nz:(v + 1) * nz]
                    ax[h, s, v, :, g:g + 8, :] = piece.reshape(half_a, 8, nz)
        core_copy(s).start()

    def line(s, hop, n, pos, view, right, left, sems, who):
        @pl.when(pos == hop)
        def _():
            for j in range(n - 1, hop - 1, -1):
                if hop > 0:
                    remote(view(acc, s, j), view(right, s, j), sems, (0, s, j), who(hop - 1)).wait_recv()
                    view(acc, s, j)[...] += view(right, s, j)[...]
                if j > hop:
                    remote(view(acc, s, j), view(right, s, j), sems, (0, s, j), who(hop + 1)).start()
        mine = n - 1 - hop

        @pl.when(pos == mine)
        def _():
            for j in range(0, mine + 1):
                if hop > 0:
                    remote(view(acc, s, j), view(left, s, j), sems, (1, s, j), who(mine + 1)).wait_recv()
                    view(acc, s, j)[...] += view(left, s, j)[...]
                if j < mine:
                    remote(view(acc, s, j), view(left, s, j), sems, (1, s, j), who(mine - 1)).start()

    def line_end(n, pos, view, right, left, sems, who):
        for p in range(n):
            @pl.when(pos == p)
            def _():
                def ends(s):
                    for j in range(p + 1, n):
                        remote(view(acc, s, j), view(right, s, j), sems, (0, s, j), who(p + 1)).wait_send()
                    for j in range(p):
                        remote(view(acc, s, j), view(left, s, j), sems, (1, s, j), who(p - 1)).wait_send()
                each(slabs, ends)

    def view_y(ref, s, j):
        return ref.at[s, :, j]

    def view_z(ref, s, j):
        return ref.at[s, :, y, j] if ref is acc else ref.at[s, :, j]

    y_args = (n_y, y, view_y, early_right, early_left, y_sem, along_y[2])
    z_args = (N_Z, z, view_z, late_right, late_left, z_sem, along_z[2])
    part = rows // n_var

    def x_copy(s, to, slot, src_var):
        return remote(acc.at[s, :, y, z, pl.ds(pl.multiple_of(to * part, part), part)],
                      pown.at[src_var, s], x_sem, (s, slot), device(pv=to))

    def stage_y(s):
        core_copy(s).wait_recv()
        own = jnp.concatenate(
            [ax[core, s, v].reshape(half_a * ny_loc, nz) for v in range(per)], axis=1)
        sib = jnp.concatenate(
            [axr[s, v].reshape(half_a * ny_loc, nz) for v in range(per)], axis=1)
        out = three(w_own, split(own)) + three(w_sib, split(sib))
        for v in range(per):
            acc[s, v] = out[:, v * nz:(v + 1) * nz].reshape(n_y, N_Z, rows, nz)

    ahead = 2
    each(ahead, stage_x)
    w_own = split(eye_kron(fy_own[:, :rb], half_a))
    fy_copy.wait()
    w_sib = split(eye_kron(fy_sib[:, :rb], half_a))
    w_v = split(kron_eye(fv_ref[...], 8))

    def x_send(s):
        for d in range(1, n_var):
            x_copy(s, lax.rem(var + d, n_var), d, var).start()
        keep = pl.ds(pl.multiple_of(var * part, part), part)
        pown[var, s] = acc[s, :, y, z, keep, :]

    plan = [(0, lambda s: line(s, 0, *y_args))]
    plan += [(h + 1, lambda s, h=h: line(s, h, *y_args)) for h in range(1, n_y)]
    plan += [(n_y + h, lambda s, h=h: line(s, h, *z_args)) for h in range(N_Z)]
    plan += [(n_y + N_Z - 1, x_send)]

    def step(t):
        @pl.when(t + ahead < slabs)
        def _():
            stage_x(t + ahead)

        @pl.when(t < slabs)
        def _():
            stage_y(t)

        for lag, act in plan:
            @pl.when((t >= lag) & (t - lag < slabs))
            def _(lag=lag, act=act):
                act(t - lag)

    each(slabs + n_y + N_Z - 1, step)

    def x_wait(s):
        for d in range(1, n_var):
            x_copy(s, lax.rem(var + d, n_var), d, lax.rem(var + n_var - d, n_var)).wait()

    each(slabs, x_wait)

    nv = n_var * slabs * per
    octets = [pown[:, :, :, o:o + 8, :].reshape(nv * 8, nz) for o in range(0, part, 8)]
    wide = three(w_v, split(jnp.concatenate(octets, axis=1)))
    wide = jnp.concatenate(
        [wide[:, k * nz:(k + 1) * nz] for k in range(len(octets))], axis=0)
    raw = exact(three(split(wide.T), split(wide)), fz_ref[...], 1, 1)

    def total(value, groups, buf, base):
        first = 0
        for n, me, who in groups:
            buf[first + me] = value
            copies = []
            for d in range(1, n):
                copies.append(remote(
                    buf.at[first + me], buf.at[first + me], red_sem,
                    (base + first + d,), who(lax.rem(me + d, n))))
                copies[-1].start()
            for copy in copies:
                copy.wait()
            value = buf[first]
            for k in range(1, n):
                value = value + buf[first + k]
            first += n
        return value

    half = nz // 2
    packed = total(
        jnp.concatenate([raw[:half], raw[half:]], axis=1), (pair, along_y, along_z), red_z, 0)
    width = raw.shape[1]
    raw = jnp.concatenate([packed[:, :width], packed[:, width:]], axis=0)
    basis_t = orth_rows(raw.T)

    tall = three(split(jnp.concatenate(octets, axis=0)), split(basis_t), 1)
    wide = split(jnp.concatenate(
        [tall[k * nv * 8:(k + 1) * nv * 8] for k in range(len(octets))], axis=1))
    cross = three(wide, wide, 1)
    cross = cross * spread((nv * 8, nv * 8), 1, 8, 1, 8)
    fold = exact(spread((nv, nv * 8), 1, nv, 8, nv), cross)
    gram_v = exact(fold, spread((nv * 8, nv), 8, nv, 1, nv))
    packed = total(
        jnp.concatenate([gram_v[k:k + 8] for k in range(0, nv, 8)], axis=1),
        (plane, along_z), red_v, red_z.shape[0])
    gram_v = jnp.concatenate([packed[:, k * nv:(k + 1) * nv] for k in range(nv // 8)], axis=0)
    proj_z_ref[...] = exact(basis_t.T, basis_t)
    new_t = orth_rows(exact(fv_ref[...], gram_v))
    proj_v_ref[...] = exact(new_t.T, new_t)
    energy = exact(new_t, gram_v) * new_t
    rms_ref[...] = jnp.sqrt(
        jnp.sum(jnp.sum(energy, axis=1, keepdims=True), axis=0, keepdims=True) * (1.0 / core_size))

    each(slabs, lambda s: core_copy(s).wait_send())
    line_end(*y_args)
    line_end(*z_args)


def per_device(n_gy, n_var, field, fx, fy, fz, fv):
    n_y = n_gy // (N_Z * N_CORE)
    v_loc, nx, ny_loc, nz = field.shape
    per = 1
    slabs = v_loc // per
    ra, rb = fx.shape[1], fy.shape[1]
    half_a = ra // N_CORE
    rows = half_a * rb // (n_y * N_Z)
    part = rows // n_var
    nv = fv.shape[0]
    slots_z = N_CORE * n_var + n_y + N_Z
    slots_v = N_CORE * n_var * n_y + N_Z
    core_size = fv.shape[1] * ra * rb * fz.shape[1]
    vmem = pl.BlockSpec(memory_space=pltpu.VMEM)
    big = (slabs, per, n_y, N_Z, rows, nz)
    small = (slabs, per, N_Z, rows, nz)
    dma = pltpu.SemaphoreType.DMA
    proj_z, proj_v, rms = pl.pallas_call(
        functools.partial(kernel, n_y, n_var, core_size),
        out_shape=(
            jax.ShapeDtypeStruct((nz, nz), F32),
            jax.ShapeDtypeStruct((nv, nv), F32),
            jax.ShapeDtypeStruct((1, 1), F32),
        ),
        in_specs=[pl.BlockSpec(memory_space=pl.ANY)] * 5,
        out_specs=(vmem, vmem, vmem),
        scratch_shapes=[
            pltpu.VMEM((slabs, per, nx, ny_loc, nz), F32),
            pltpu.VMEM((N_CORE, slabs, per, half_a, ny_loc, nz), F32),
            pltpu.VMEM((slabs, per, half_a, ny_loc, nz), F32),
            pltpu.VMEM((ny_loc, 128), F32),
            pltpu.VMEM((ny_loc, 128), F32),
            pltpu.VMEM(big, F32),
            pltpu.VMEM(big, F32),
            pltpu.VMEM(big, F32),
            pltpu.VMEM(small, F32),
            pltpu.VMEM(small, F32),
            pltpu.VMEM((n_var, slabs, per, part, nz), F32),
            pltpu.VMEM((slots_z, nz // 2, 2 * fz.shape[1]), F32),
            pltpu.VMEM((slots_v, 8, nv * nv // 8), F32),
            pltpu.VMEM(fx.shape[::-1], F32),
            pltpu.VMEM(fy.shape, F32),
            pltpu.VMEM(fz.shape[::-1], F32),
            pltpu.VMEM(fv.shape[::-1], F32),
            dma((slabs,)),
            dma((4,)),
            dma((2, 1)),
            dma((2, slabs)),
            dma((2, 2, slabs, n_y)),
            dma((2, 2, slabs, N_Z)),
            dma((2, slabs, n_var)),
            dma((2, slots_z + slots_v)),
        ],
        compiler_params=pltpu.CompilerParams(
            collective_id=0, has_side_effects=True, vmem_limit_bytes=52 * 2**20),
        cost_estimate=pl.CostEstimate(
            flops=10**10, bytes_accessed=4 * v_loc * nx * ny_loc * nz, transcendentals=0),
    )(field, fx.T, fy, fz.T, fv.T)
    return proj_z, proj_v, rms[0, 0]


def solution(mesh):
    in_specs = (P("var", None, "gy", None), P(), P("gy", None), P(), P())
    return jax.shard_map(
        functools.partial(per_device, mesh.shape["gy"], mesh.shape["var"]),
        mesh=mesh, in_specs=in_specs, out_specs=(P(), P(), P()), check_vma=False,
    )
```
